512 devices in a mesh: ray: 32 (over z, y_lo), cell: 16 (over x, y_hi, core).
Axes of the slice: x: 4, y: 4 (y_hi: 2, y_lo: 2; y = y_hi * 2 + y_lo), z: 16, core: 2. Of those that a mesh axis runs over, the one named last changes fastest.
Arguments:
- tile_values: bfloat16 [256, 16, 4, 128, 128], P('ray', 'cell'), may hold values from -0.375 to 0.375
- tile_cols: int32 [256, 16, 4], P('ray', 'cell'), may hold values from 0 to 3, as said below
- tile_count: int32 [256, 16], P('ray', 'cell'), may hold values from 0 to 4
- ray_weight: float32 [32768], P('ray'), may hold values from 0.2 to 5
Outputs:
- hessian_blocks: float32 [4, 16, 512, 512], P(None, 'cell', 'ray')
The draws below stay inside these ranges and needn't reach their ends.
Inputs may be any that keep to these rules, and one draw needn't show every extreme that they name: `tile_cols`: within one ray tile and panel the 4 slots name different cell tiles; slots at or beyond tile_count are padding and their tiles are not part of the Jacobian.
All inputs are finite; a program needn't handle non-finite values.
Results may differ from the reference program's by a relative error of at most 0.00094.
Values may be sent and summed in bfloat16 or wider, within the bound.
A program may use at most 64 MiB of HBM per device.

```python
import math
import jax
import jax.numpy as jnp
from jax import lax

TILE = 128
K = 4
STEPS = 4
CT = 4
RAY_TILES = 256
RAYS = 32768
N_CELL = 16


def draw_tile_cols(key, part):
    scores = jax.random.randint(key, (RAY_TILES, N_CELL, CT), 0, 1 << 20, dtype=jnp.int32) * CT + jnp.arange(CT, dtype=jnp.int32)
    order = jnp.argsort(scores, axis=-1)
    return order[..., :K].astype(jnp.int32)


def with_ends(result, rng, low, largest):
    longest = result.shape.index(max(result.shape))
    spots = []
    for shift in (0, 1):
        where = [jax.random.randint(jax.random.fold_in(rng, axis), (), 0, length) for axis, length in enumerate(result.shape)]
        where[longest] = (where[longest] + shift) % result.shape[longest]
        spots.append(tuple(where))
    return result.at[spots[0]].set(low).at[spots[1]].set(largest)


def shard_levels(own_key, dims, cuts, low, largest):
    gain, own = 1.0, jax.random.fold_in(own_key, 6)
    for position, shards_of in cuts:
        steps = jnp.exp(jax.random.uniform(jax.random.fold_in(own, position), (shards_of,), jnp.float32, low / len(cuts), largest / len(cuts)))
        gain = gain * jnp.repeat(steps, dims[position] // shards_of).reshape([-1 if axis == position else 1 for axis in range(len(dims))])
    return gain


def bell_draw(own_key, extent, width, reach, cuts=(), kind=jnp.bfloat16):
    array = jax.random.normal(own_key, extent, jnp.float32) * width
    if len(cuts) > 0:
        array = shard_levels(own_key, extent, cuts, -0.22, 0.18) * array
    return jnp.clip(array, min=-reach, max=reach).astype(kind)


def setup_inputs(seed: int = 0) -> dict:
    splits = jax.random.split(jax.random.key(seed), 5)
    tile_values = bell_draw(splits[0], (RAY_TILES, N_CELL, K, TILE, TILE), (RAYS // 128) ** -0.5, 0.375, ((0, 32), (1, 16)))
    tile_cols = draw_tile_cols(jax.random.fold_in(splits[4], 71), 0)
    tile_count = with_ends(jax.random.randint(splits[2], (RAY_TILES, N_CELL), 0, K + 1), jax.random.fold_in(splits[2], 1), 0, K).astype(jnp.int32)
    ray_weight = jnp.clip(jnp.exp(math.log(5.0) - 3.218876 * jax.random.uniform(splits[3], (RAYS,), jnp.float32) ** shard_levels(splits[3], (RAYS,), ((0, 32),), -0.2, 0.2)), 0.2, 5.0)
    return {"tile_values": tile_values, "tile_cols": tile_cols, "tile_count": tile_count, "ray_weight": ray_weight}


def place_table(columns, counts, panel_tiles):
    slot_index = jnp.arange(columns.shape[-1], dtype=jnp.int32)
    is_live = slot_index[None, :] < counts[:, None]
    is_match = columns[:, :, None] == jnp.arange(panel_tiles, dtype=jnp.int32)[None, None, :]
    return (is_match & is_live[:, :, None]).astype(jnp.float32)


def placed_rows(values, table):
    spread = jnp.einsum('tki,tkra->tria', table, values.astype(jnp.float32), precision=lax.Precision.HIGHEST)
    return spread.reshape(-1, CT * TILE)


def reference(tile_values, tile_cols, tile_count, ray_weight):
    results = []
    for cycle_step in range(STEPS):
        def one_panel(panel):
            source = (panel - cycle_step) % N_CELL
            own_values = lax.dynamic_index_in_dim(tile_values, panel, 1, keepdims=False)
            own_cols = lax.dynamic_index_in_dim(tile_cols, panel, 1, keepdims=False)
            own_count = lax.dynamic_index_in_dim(tile_count, panel, 1, keepdims=False)
            visit_values = lax.dynamic_index_in_dim(tile_values, source, 1, keepdims=False)
            visit_cols = lax.dynamic_index_in_dim(tile_cols, source, 1, keepdims=False)
            visit_count = lax.dynamic_index_in_dim(tile_count, source, 1, keepdims=False)
            own_weighted = (ray_weight.reshape(RAY_TILES, 1, TILE, 1) * own_values.astype(jnp.float32)).astype(jnp.bfloat16)
            own_placed = placed_rows(own_weighted, place_table(own_cols, own_count, CT))
            visit_placed = placed_rows(visit_values, place_table(visit_cols, visit_count, CT))
            return lax.dot_general(own_placed, visit_placed, (((0,), (0,)), ((), ())), precision=lax.Precision.HIGHEST)

        results.append(lax.map(one_panel, jnp.arange(N_CELL, dtype=jnp.int32)))
    return jnp.stack(results)
```

```python
import functools

import jax
import jax.numpy as jnp
from jax import lax
from jax.experimental import pallas as pl
from jax.experimental.pallas import tpu as pltpu
from jax.sharding import PartitionSpec as P

MESH = pl.DeviceIdType.MESH
TILE = 128
K = 4
CT = 4
FULL = 32700.0
STEP = 64.0


def streams_of(size, stride, mirror):
    found = []
    half = size // 2
    for sign, reach in ((1, half), (-1, size - 1 - half)):
        for rest in range(stride):
            path = [o for o in range(reach, 0, -1) if o % stride == rest % stride]
            if path:
                found.append([o * sign * (-1 if mirror else 1) for o in path])
    return found


class Stage:
    def __init__(self, name, items, streams, refs):
        self.name, self.items, self.streams, self.refs = name, items, streams, refs
        self.first = []
        count = 0
        for path in streams:
            self.first.append(count)
            count += len(path)
        self.messages = count
        self.steps = max(len(path) for path in streams)


PLAN = (("a", 4, 2, False), ("b", 4, 2, True), ("c0", 2, 2, False), ("c1", 2, 2, True), ("c2", 2, 2, False), ("c3", 2, 2, True))


def coded(x):
    largest = jnp.max(jnp.max(jnp.abs(x), axis=0), axis=0, keepdims=True)
    power = jnp.floor(jnp.log2(jnp.maximum(largest, 1e-30)) * STEP) + 1.0
    codes = jnp.round(x * (jnp.exp2(power * (-1.0 / STEP)) * FULL)[None])
    return codes.astype(jnp.int32).astype(jnp.int16), power


def kernel(nz, plan, values, cols, count, weight, out, *scratch):
    n_stages = len(plan)
    (own_v, own_wt, got_z, got_sib, got_r, in_send, in_recv) = scratch[:7]
    per = scratch[7 : 7 + 8 * n_stages]
    (b_out, b_in, b_send, b_recv) = scratch[7 + 8 * n_stages :]
    stages = []
    for i, (name, items, stride, mirror) in enumerate(plan):
        stages.append(Stage(name, items, streams_of(nz, stride, mirror), per[8 * i : 8 * i + 8]))

    p = lax.axis_index("cell")
    ray = lax.axis_index("ray")
    n_cell = lax.axis_size("cell")
    z, yl = ray // 2, ray % 2
    odd = p % 2
    chunk = CT * TILE // nz

    def at_cell(shift):
        return {"ray": ray, "cell": lax.rem(p + shift + n_cell, n_cell)}

    def at_z(shift):
        return {"ray": lax.rem(z + shift + nz, nz) * 2 + yl, "cell": p}

    sibling = {"ray": ray, "cell": p + 1 - 2 * odd}
    across = {"ray": ray + 1 - 2 * yl, "cell": p}
    r_target = at_cell(2 * odd - 3)
    r_source = at_cell(2 * odd + 1)
    third = at_cell(6 * odd - 3)

    shifts = set()
    for stage in stages:
        for path in stage.streams:
            for i, o in enumerate(path):
                d = (path[i + 1] if i + 1 < len(path) else 0) - o
                shifts.update((d, -d))
    peers = [sibling, at_cell(2), at_cell(-2), third, across] + [at_z(d) for d in sorted(shifts)]
    barrier = pltpu.get_barrier_semaphore()
    for peer in peers:
        pl.semaphore_signal(barrier, inc=1, device_id=peer, device_id_type=MESH)

    row_tiles = values.shape[0]
    started = []

    def send(src, dst, ssem, rsem, to):
        copy = pltpu.make_async_remote_copy(
            src_ref=src, dst_ref=dst, send_sem=ssem, recv_sem=rsem, device_id=to, device_id_type=MESH
        )
        copy.start()
        started.append(copy)
        return copy

    def await_recv(dst, ssem, rsem):
        pltpu.make_async_remote_copy(
            src_ref=dst, dst_ref=dst, send_sem=ssem, recv_sem=rsem, device_id=sibling, device_id_type=MESH
        ).wait_recv()

    def placed(t, i):
        slot, live = jnp.int32(0), jnp.int32(0)
        for k in range(K):
            here = jnp.where((cols[t, k] == i) & (k < count[t]), 1, 0)
            slot += k * here
            live += here
        return values[t, slot].astype(jnp.float32) * live.astype(jnp.float32)

    def place(t, carry):
        for i in range(CT):
            own_v[i, pl.ds(pl.multiple_of(t * TILE, TILE), TILE), :] = placed(t, i).astype(jnp.bfloat16)
        return carry

    lax.fori_loop(0, row_tiles, place, 0)
    pl.semaphore_wait(barrier, len(peers))

    for j in range(CT):
        send(own_v.at[j], got_z.at[j], in_send.at[j], in_recv.at[j], at_cell(2))

    def weigh(t, carry):
        spot = pl.ds(pl.multiple_of(t * TILE, TILE), TILE)
        row = weight[pl.ds(t, 1), :]
        for i in range(CT):
            turned = own_v[i, spot, :].astype(jnp.float32).T
            own_wt[i * TILE : (i + 1) * TILE, spot] = (turned * row).astype(jnp.bfloat16)
        return carry

    lax.fori_loop(0, row_tiles, weigh, 0)
    send(own_wt, got_r, in_send.at[8], in_recv.at[8], r_target)

    def multiply(stage, left, pieces):
        part = stage.refs[0]

        def rows(m, carry):
            spot = pl.ds(pl.multiple_of(m * TILE, TILE), TILE)
            lhs = left[spot, :]
            for i in range(0, len(pieces), 2):
                rhs = jnp.concatenate([pieces[i][...], pieces[i + 1][...]], axis=1)
                got = jnp.dot(lhs, rhs, preferred_element_type=jnp.float32)
                part[i, spot, :] = got[:, :TILE]
                part[i + 1, spot, :] = got[:, TILE:]
            return carry

        lax.fori_loop(0, CT, rows, 0)

    def own_part(stage, dest):
        return stage.refs[0][:, pl.ds(pl.multiple_of(dest * chunk, chunk), chunk), :]

    def arrived(stage, m):
        part, sbuf, rbuf, ssem, rsem = stage.refs[:5]
        await_recv(rbuf.at[m], ssem.at[m], rsem.at[m])
        rows = stage.items * chunk
        codes = rbuf[m, 0:rows, :].astype(jnp.int32).astype(jnp.float32)
        power = rbuf[m, rows : rows + 16, :].astype(jnp.int32).astype(jnp.float32)[0:1]
        scale = jnp.exp2(power * (1.0 / STEP)) * (1.0 / FULL)
        return (codes * scale).reshape(stage.items, chunk, TILE)

    def step(stage, s):
        part, sbuf, rbuf, ssem, rsem = stage.refs[:5]
        rows = stage.items * chunk
        for path, first in zip(stage.streams, stage.first):
            if s >= len(path):
                continue
            o, m = path[s], first + s
            x = own_part(stage, lax.rem(z - o + nz, nz))
            if s > 0:
                x = x + arrived(stage, m - 1)
            codes, power = coded(x)
            sbuf[m, 0:rows, :] = codes.reshape(rows, TILE)
            sbuf[m, rows : rows + 16, :] = jnp.broadcast_to(power, (16, TILE)).astype(jnp.int32).astype(jnp.int16)
            ahead = path[s + 1] if s + 1 < len(path) else 0
            send(sbuf.at[m], rbuf.at[m], ssem.at[m], rsem.at[m], at_z(ahead - o))

    def gather(stage):
        part, sbuf, rbuf, ssem, rsem, total, other, swap = stage.refs
        x = own_part(stage, z)
        for path, first in zip(stage.streams, stage.first):
            x = x + arrived(stage, first + len(path) - 1)
        half = chunk // 2
        total[0] = x[:, :half]
        total[1] = x[:, half:]
        send(total.at[1 - yl], other, swap.at[0], swap.at[1], across)

    def finish(stage):
        part, sbuf, rbuf, ssem, rsem, total, other, swap = stage.refs
        await_recv(other, swap.at[0], swap.at[1])
        return total[yl] + other[...]

    a, b = stages[0], stages[1]
    visits = stages[2:]
    sib_s = 1 + 2 * odd
    b_s = 3 - 2 * odd

    def start_a():
        multiply(a, own_wt, [own_v.at[j] for j in range(CT)])

    def start_b():
        await_recv(got_r, in_send.at[8], in_recv.at[8])
        multiply(b, got_r, [own_v.at[j] for j in range(CT)])

    def pass_on(j):
        await_recv(got_z.at[j], in_send.at[j], in_recv.at[j])
        send(got_z.at[j], got_sib.at[j], in_send.at[4 + j], in_recv.at[4 + j], sibling)

    def start_c(j):
        await_recv(got_sib.at[j], in_send.at[4 + j], in_recv.at[4 + j])
        multiply(visits[j], own_wt, [got_z.at[j], got_sib.at[j]])

    def finish_a():
        x = finish(a)
        for i in range(CT):
            out[0, 0, :, i * TILE : (i + 1) * TILE] = x[i]

    def finish_b():
        b_out[...] = finish(b)
        send(b_out, b_in, b_send, b_recv, r_source)

    def take_b():
        await_recv(b_in, b_send, b_recv)
        for i in range(CT):
            out[b_s, 0, :, i * TILE : (i + 1) * TILE] = b_in[i]

    def finish_c(j):
        x = finish(visits[j])
        out[2, 0, :, j * TILE : (j + 1) * TILE] = x[0]
        out[sib_s, 0, :, j * TILE : (j + 1) * TILE] = x[1]

    events = []
    tick = 4.2

    def run(stage, ready, begin, end):
        events.append((ready, begin))
        for s in range(stage.steps):
            events.append((ready + 0.1 + tick * s, functools.partial(step, stage, s)))
        events.append((ready + 0.1 + tick * stage.steps, functools.partial(gather, stage)))
        events.append((ready + 3.5 + tick * stage.steps, end))

    run(a, 0.0, start_a, finish_a)
    run(b, 14.0, start_b, finish_b)
    events.append((14.0 + 7.0 + tick * b.steps, take_b))
    for j in range(CT):
        ready = 4.0 + 5.3 * (j + 1)
        events.append((ready, functools.partial(pass_on, j)))
        run(visits[j], ready + 2.0, functools.partial(start_c, j), functools.partial(finish_c, j))
    for _, event in sorted(events, key=lambda e: e[0]):
        event()
    for copy in started:
        copy.wait_send()


def body(nz, plan, tile_values, tile_cols, tile_count, ray_weight):
    row_tiles = tile_values.shape[0]
    rays = row_tiles * TILE
    chunk = CT * TILE // nz
    bf16, f32 = jnp.bfloat16, jnp.float32
    dma = pltpu.SemaphoreType.DMA
    scratch = [
        pltpu.VMEM((CT, rays, TILE), bf16),
        pltpu.VMEM((CT * TILE, rays), bf16),
        pltpu.VMEM((CT, rays, TILE), bf16),
        pltpu.VMEM((CT, rays, TILE), bf16),
        pltpu.VMEM((CT * TILE, rays), bf16),
        dma((9,)),
        dma((9,)),
    ]
    for name, items, stride, mirror in plan:
        count = nz - 1
        rows = items * chunk + 16
        scratch += [
            pltpu.VMEM((items, CT * TILE, TILE), f32),
            pltpu.VMEM((count, rows, TILE), jnp.int16),
            pltpu.VMEM((count, rows, TILE), jnp.int16),
            dma((count,)),
            dma((count,)),
            pltpu.VMEM((2, items, chunk // 2, TILE), f32),
            pltpu.VMEM((items, chunk // 2, TILE), f32),
            dma((2,)),
        ]
    scratch += [
        pltpu.VMEM((CT, chunk // 2, TILE), f32),
        pltpu.VMEM((CT, chunk // 2, TILE), f32),
        dma,
        dma,
    ]
    vmem, smem = pl.BlockSpec(memory_space=pltpu.VMEM), pl.BlockSpec(memory_space=pltpu.SMEM)
    return pl.pallas_call(
        functools.partial(kernel, nz, plan),
        out_shape=jax.ShapeDtypeStruct((4, 1, chunk // 2, CT * TILE), f32),
        in_specs=[vmem, smem, smem, vmem],
        out_specs=vmem,
        scratch_shapes=scratch,
        compiler_params=pltpu.CompilerParams(
            collective_id=0, has_side_effects=True, vmem_limit_bytes=48 << 20
        ),
    )(
        tile_values.reshape(row_tiles, K, TILE, TILE),
        tile_cols.reshape(row_tiles, K),
        tile_count.reshape(row_tiles),
        ray_weight.reshape(row_tiles, TILE),
    )


def solution(mesh):
    return jax.shard_map(
        functools.partial(body, mesh.shape["ray"] // 2, PLAN),
        mesh=mesh,
        in_specs=(P("ray", "cell", None, None, None), P("ray", "cell", None), P("ray", "cell"), P("ray")),
        out_specs=P(None, "cell", "ray", None),
        check_vma=False,
    )
```

```python
import functools

import jax
import jax.numpy as jnp
from jax import lax
from jax.experimental import pallas as pl
from jax.experimental.pallas import tpu as pltpu
from jax.sharding import PartitionSpec as P

MESH = pl.DeviceIdType.MESH
TILE = 128
K = 4
CT = 4
FULL = 32700.0
STEP = 64.0


def streams_of(size, stride, mirror):
    found = []
    half = size // 2
    for sign, reach in ((1, half), (-1, size - 1 - half)):
        for rest in range(stride):
            path = [o for o in range(reach, 0, -1) if o % stride == rest % stride]
            if path:
                found.append([o * sign * (-1 if mirror else 1) for o in path])
    return found


class Stage:
    def __init__(self, items, size, stride, mirror, near_first, refs):
        self.items, self.near_first, self.refs = items, near_first, refs
        self.paths = streams_of(size, stride, mirror)
        self.steps = []
        self.place = {}
        self.count = 0
        self.widest = 1
        for s in range(max(len(path) for path in self.paths)):
            groups = {}
            for k, path in enumerate(self.paths):
                if s < len(path):
                    ahead = path[s + 1] if s + 1 < len(path) else 0
                    groups.setdefault(ahead - path[s], []).append(k)
            found = []
            for hop, members in groups.items():
                for slot, k in enumerate(members):
                    self.place[k, s] = (self.count, slot, len(members))
                self.widest = max(self.widest, len(members))
                found.append((self.count, hop, members))
                self.count += 1
            self.steps.append(found)
        self.hops = {hop for found in self.steps for _, hop, _ in found}
        self.seen = set()


PLAN = (
    ("a", 4, 1, False, False),
    ("b", 4, 1, True, False),
    ("c0", 2, 1, False, False),
    ("c1", 2, 1, True, False),
    ("c2", 2, 2, False, True),
    ("c3", 2, 2, True, True),
)
TICK = {1: 3.5, 2: 4.1, 4: 5.5, 8: 9.0}


def coded(x):
    largest = jnp.max(jnp.max(jnp.abs(x), axis=0), axis=0, keepdims=True)
    power = jnp.floor(jnp.log2(jnp.maximum(largest, 1e-30)) * STEP) + 1.0
    codes = jnp.round(x * (jnp.exp2(power * (-1.0 / STEP)) * FULL)[None])
    return codes.astype(jnp.int32).astype(jnp.int16), power


def kernel(nz, plan, values, cols, count, weight, out, *scratch):
    (held, in_copy, own_v, own_wt, got_z, got_sib, got_r, in_send, in_recv) = scratch[:9]
    (b_out, b_in, b_send, b_recv) = scratch[-4:]
    stages = []
    for i, (name, items, stride, mirror, near_first) in enumerate(plan):
        stages.append(Stage(items, nz, stride, mirror, near_first, scratch[9 + 8 * i : 17 + 8 * i]))

    fetch = pltpu.make_async_copy(values, held, in_copy)
    fetch.start()
    p = lax.axis_index("cell")
    ray = lax.axis_index("ray")
    n_cell = lax.axis_size("cell")
    z, yl = ray // 2, ray % 2
    odd = p % 2
    chunk = CT * TILE // nz
    half = chunk // 2

    def at_cell(shift):
        return {"ray": ray, "cell": lax.rem(p + shift + n_cell, n_cell)}

    def at_z(shift):
        return {"ray": lax.rem(z + shift + nz, nz) * 2 + yl, "cell": p}

    sibling = {"ray": ray, "cell": p + 1 - 2 * odd}
    across = {"ray": ray + 1 - 2 * yl, "cell": p}
    r_target = at_cell(2 * odd - 3)
    r_source = at_cell(2 * odd + 1)
    third = at_cell(6 * odd - 3)

    shifts = set()
    for stage in stages:
        for hop in stage.hops:
            shifts.update((hop, -hop))
    peers = [sibling, at_cell(2), at_cell(-2), third, across] + [at_z(d) for d in sorted(shifts)]
    barrier = pltpu.get_barrier_semaphore()
    for peer in peers:
        pl.semaphore_signal(barrier, inc=1, device_id=peer, device_id_type=MESH)

    row_tiles = values.shape[0]
    started = []

    def send(src, dst, ssem, rsem, to):
        copy = pltpu.make_async_remote_copy(
            src_ref=src, dst_ref=dst, send_sem=ssem, recv_sem=rsem, device_id=to, device_id_type=MESH
        )
        copy.start()
        started.append(copy)
        return copy

    def await_recv(dst, ssem, rsem):
        pltpu.make_async_remote_copy(
            src_ref=dst, dst_ref=dst, send_sem=ssem, recv_sem=rsem, device_id=sibling, device_id_type=MESH
        ).wait_recv()

    def placed(t, i):
        slot, live = jnp.int32(0), jnp.int32(0)
        for k in range(K):
            here = jnp.where((cols[k, t] == i) & (k < count[t]), 1, 0)
            slot += k * here
            live += here
        return held[t, slot].astype(jnp.float32) * live.astype(jnp.float32)

    def place(t, carry):
        for i in range(CT):
            own_v[i, pl.ds(pl.multiple_of(t * TILE, TILE), TILE), :] = placed(t, i).astype(jnp.bfloat16)
        return carry

    fetch.wait()
    lax.fori_loop(0, row_tiles, place, 0)
    pl.semaphore_wait(barrier, len(peers))

    for j in range(CT):
        send(own_v.at[j], got_z.at[j], in_send.at[j], in_recv.at[j], at_cell(2))

    def weigh(t, carry):
        spot = pl.ds(pl.multiple_of(t * TILE, TILE), TILE)
        row = weight[pl.ds(t, 1), :]
        for i in range(CT):
            turned = own_v[i, spot, :].astype(jnp.float32).T
            own_wt[i * TILE : (i + 1) * TILE, spot] = (turned * row).astype(jnp.bfloat16)
        return carry

    lax.fori_loop(0, row_tiles, weigh, 0)
    send(own_wt, got_r, in_send.at[8], in_recv.at[8], r_target)

    def multiply(stage, left, pieces):
        part = stage.refs[0]

        def rows(m, carry):
            spot = pl.ds(pl.multiple_of(m * TILE, TILE), TILE)
            lhs = left[spot, :]
            for i in range(0, len(pieces), 2):
                rhs = jnp.concatenate([pieces[i][...], pieces[i + 1][...]], axis=1)
                got = jnp.dot(lhs, rhs, preferred_element_type=jnp.float32)
                for e in (0, 1):
                    tile = got[:, e * TILE : (e + 1) * TILE]
                    if not stage.near_first:
                        part[0, i + e, spot, :] = tile
                        continue
                    for q in range(TILE // half):
                        to = pl.ds(pl.multiple_of(m * (TILE // 2) + q // 2 * half, half), half)
                        part[q % 2, i + e, to, :] = tile[q * half : (q + 1) * half]
            return carry

        lax.fori_loop(0, CT, rows, 0)

    def decoded(buf, m, slot, width, rows):
        first = 16 + slot * rows
        codes = buf[m, first : first + rows, :].astype(jnp.int32).astype(jnp.float32)
        power = buf[m, 0:16, :].astype(jnp.int32).astype(jnp.float32)
        at = slot * (16 // width)
        return codes * (jnp.exp2(power[at : at + 1] * (1.0 / STEP)) * (1.0 / FULL))

    def encode(buf, m, pieces):
        lines = lax.broadcasted_iota(jnp.int32, (16, TILE), 0)
        for slot, x in enumerate(pieces):
            codes, power = coded(x)
            rows = x.shape[0] * x.shape[1]
            buf[m, 16 + slot * rows : 16 + (slot + 1) * rows, :] = codes.reshape(rows, TILE)
            power = jnp.broadcast_to(power, (16, TILE))
            powers = power if slot == 0 else jnp.where(lines >= slot * (16 // len(pieces)), power, powers)
        buf[m, 0:16, :] = powers.astype(jnp.int32).astype(jnp.int16)

    def own_part(stage, dest):
        part = stage.refs[0]
        if stage.near_first:
            return part[yl, :, pl.ds(pl.multiple_of(dest * half, half), half), :]
        return part[0, :, pl.ds(pl.multiple_of(dest * chunk, chunk), chunk), :]

    def arrived(stage, k, s):
        part, sbuf, rbuf, ssem, rsem = stage.refs[:5]
        m, slot, width = stage.place[k, s]
        tall = half if stage.near_first else chunk
        rows = stage.items * tall
        if m not in stage.seen:
            stage.seen.add(m)
            spot = rbuf.at[m, pl.ds(0, 16 + width * rows)]
            await_recv(spot, ssem.at[m], rsem.at[m])
        return decoded(rbuf, m, slot, width, rows).reshape(stage.items, tall, TILE)

    def step(stage, s):
        part, sbuf, rbuf, ssem, rsem = stage.refs[:5]
        for m, hop, members in stage.steps[s]:
            pieces = []
            for k in members:
                x = own_part(stage, lax.rem(z - stage.paths[k][s] + nz, nz))
                pieces.append(x if s == 0 else x + arrived(stage, k, s - 1))
            encode(sbuf, m, pieces)
            size = 16 + len(members) * pieces[0].shape[0] * pieces[0].shape[1]
            spot = pl.ds(0, size)
            send(sbuf.at[m, spot], rbuf.at[m, spot], ssem.at[m], rsem.at[m], at_z(hop))

    def summed(stage):
        x = own_part(stage, z)
        for k, path in enumerate(stage.paths):
            x = x + arrived(stage, k, len(path) - 1)
        return x

    def cross(stage):
        part, near_out, near_in, swap = stage.refs[0], stage.refs[5], stage.refs[6], stage.refs[7]
        encode(near_out, 0, [part[1 - yl]])
        send(near_out, near_in, swap.at[0], swap.at[1], across)

    def merge(stage):
        part, near_in, swap = stage.refs[0], stage.refs[6], stage.refs[7]
        await_recv(near_in, swap.at[0], swap.at[1])
        rows = stage.items * half * nz
        part[yl] = part[yl] + decoded(near_in, 0, 0, 1, rows).reshape(stage.items, half * nz, TILE)

    def gather(stage):
        total, other, swap = stage.refs[5:]
        x = summed(stage)
        total[0] = x[:, :half]
        total[1] = x[:, half:]
        send(total.at[1 - yl], other, swap.at[0], swap.at[1], across)

    def finish(stage):
        if stage.near_first:
            return summed(stage)
        total, other, swap = stage.refs[5:]
        await_recv(other, swap.at[0], swap.at[1])
        return total[yl] + other[...]

    a, b = stages[0], stages[1]
    visits = stages[2:]
    sib_s = 1 + 2 * odd
    b_s = 3 - 2 * odd

    def start_a():
        multiply(a, own_wt, [own_v.at[j] for j in range(CT)])

    def start_b():
        await_recv(got_r, in_send.at[8], in_recv.at[8])
        multiply(b, got_r, [own_v.at[j] for j in range(CT)])

    def pass_on(j):
        await_recv(got_z.at[j], in_send.at[j], in_recv.at[j])
        send(got_z.at[j], got_sib.at[j], in_send.at[4 + j], in_recv.at[4 + j], sibling)

    def start_c(j):
        await_recv(got_sib.at[j], in_send.at[4 + j], in_recv.at[4 + j])
        multiply(visits[j], own_wt, [got_z.at[j], got_sib.at[j]])

    def finish_a():
        x = finish(a)
        for i in range(CT):
            out[0, 0, :, i * TILE : (i + 1) * TILE] = x[i]

    def finish_b():
        b_out[...] = finish(b)
        send(b_out, b_in, b_send, b_recv, r_source)

    def take_b():
        await_recv(b_in, b_send, b_recv)
        for i in range(CT):
            out[b_s, 0, :, i * TILE : (i + 1) * TILE] = b_in[i]

    def finish_c(j):
        x = finish(visits[j])
        out[2, 0, :, j * TILE : (j + 1) * TILE] = x[0]
        out[sib_s, 0, :, j * TILE : (j + 1) * TILE] = x[1]

    events = []

    def run(stage, stride, ready, begin, end):
        events.append((ready, begin))
        tick = TICK[stride]
        if stage.near_first:
            events.append((ready + 0.01, functools.partial(cross, stage)))
            events.append((ready + 4.5, functools.partial(merge, stage)))
            ready += 4.5
        for s in range(len(stage.steps)):
            events.append((ready + 0.1 + tick * s, functools.partial(step, stage, s)))
        ready += 0.1 + tick * len(stage.steps)
        if not stage.near_first:
            events.append((ready, functools.partial(gather, stage)))
            ready += 3.4
        events.append((ready, end))
        return ready

    run(a, plan[0][2], 0.0, start_a, finish_a)
    done = run(b, plan[1][2], 14.0, start_b, finish_b)
    events.append((done + 3.4, take_b))
    for j in range(CT):
        ready = 3.0 + 5.1 * (j + 1)
        events.append((ready, functools.partial(pass_on, j)))
        run(visits[j], plan[2 + j][2], ready + 1.7, functools.partial(start_c, j), functools.partial(finish_c, j))
    for _, event in sorted(events, key=lambda e: e[0]):
        event()
    for copy in started:
        copy.wait_send()


def body(nz, plan, tile_values, tile_cols, tile_count, ray_weight):
    row_tiles = tile_values.shape[0]
    rays = row_tiles * TILE
    chunk = CT * TILE // nz
    bf16, f32 = jnp.bfloat16, jnp.float32
    dma = pltpu.SemaphoreType.DMA
    scratch = [
        pltpu.VMEM((row_tiles, K, TILE, TILE), bf16),
        dma,
        pltpu.VMEM((CT, rays, TILE), bf16),
        pltpu.VMEM((CT * TILE, rays), bf16),
        pltpu.VMEM((CT, rays, TILE), bf16),
        pltpu.VMEM((CT, rays, TILE), bf16),
        pltpu.VMEM((CT * TILE, rays), bf16),
        dma((9,)),
        dma((9,)),
    ]
    half = chunk // 2
    for name, items, stride, mirror, near_first in plan:
        stage = Stage(items, nz, stride, mirror, near_first, None)
        rows = 16 + stage.widest * items * (half if near_first else chunk)
        near = (1, 16 + items * half * nz, TILE)
        scratch += [
            pltpu.VMEM((2, items, half * nz, TILE) if near_first else (1, items, chunk * nz, TILE), f32),
            pltpu.VMEM((stage.count, rows, TILE), jnp.int16),
            pltpu.VMEM((stage.count, rows, TILE), jnp.int16),
            dma((stage.count,)),
            dma((stage.count,)),
            pltpu.VMEM(near, jnp.int16) if near_first else pltpu.VMEM((2, items, half, TILE), f32),
            pltpu.VMEM(near, jnp.int16) if near_first else pltpu.VMEM((items, half, TILE), f32),
            dma((2,)),
        ]
    scratch += [
        pltpu.VMEM((CT, chunk // 2, TILE), f32),
        pltpu.VMEM((CT, chunk // 2, TILE), f32),
        dma,
        dma,
    ]
    vmem, smem = pl.BlockSpec(memory_space=pltpu.VMEM), pl.BlockSpec(memory_space=pltpu.SMEM)
    return pl.pallas_call(
        functools.partial(kernel, nz, plan),
        out_shape=jax.ShapeDtypeStruct((4, 1, chunk // 2, CT * TILE), f32),
        in_specs=[pl.BlockSpec(memory_space=pltpu.HBM), smem, smem, vmem],
        out_specs=vmem,
        scratch_shapes=scratch,
        compiler_params=pltpu.CompilerParams(
            collective_id=0, has_side_effects=True, vmem_limit_bytes=62 << 20
        ),
    )(
        tile_values.reshape(row_tiles, K, TILE, TILE),
        tile_cols.reshape(row_tiles, K).T,
        tile_count.reshape(row_tiles),
        ray_weight.reshape(row_tiles, TILE),
    )


def solution(mesh):
    return jax.shard_map(
        functools.partial(body, mesh.shape["ray"] // 2, PLAN),
        mesh=mesh,
        in_specs=(P("ray", "cell", None, None, None), P("ray", "cell", None), P("ray", "cell"), P("ray")),
        out_specs=P(None, "cell", "ray", None),
        check_vma=False,
    )
```

```python
import functools

import jax
import jax.numpy as jnp
from jax import lax
from jax.experimental import pallas as pl
from jax.experimental.pallas import tpu as pltpu
from jax.sharding import PartitionSpec as P

MESH = pl.DeviceIdType.MESH
TILE = 128
K = 4
CT = 4
FULL = 32700.0
STEP = 64.0


def streams_of(size, stride, mirror):
    found = []
    half = size // 2
    for sign, reach in ((1, half), (-1, size - 1 - half)):
        for rest in range(stride):
            path = [o for o in range(reach, 0, -1) if o % stride == rest % stride]
            if path:
                found.append([o * sign * (-1 if mirror else 1) for o in path])
    return found


class Stage:
    def __init__(self, items, size, stride, mirror, near_first, refs):
        self.items, self.near_first, self.refs = items, near_first, refs
        self.paths = streams_of(size, stride, mirror)
        self.steps = []
        self.place = {}
        self.count = 0
        self.widest = 1
        for s in range(max(len(path) for path in self.paths)):
            groups = {}
            for k, path in enumerate(self.paths):
                if s < len(path):
                    ahead = path[s + 1] if s + 1 < len(path) else 0
                    groups.setdefault(ahead - path[s], []).append(k)
            found = []
            for hop, members in groups.items():
                for slot, k in enumerate(members):
                    self.place[k, s] = (self.count, slot, len(members))
                self.widest = max(self.widest, len(members))
                found.append((self.count, hop, members))
                self.count += 1
            self.steps.append(found)
        self.hops = {hop for found in self.steps for _, hop, _ in found}
        self.seen = set()


PLAN = (('a', 4, 1, False, False), ('b0', 4, 1, True, False), ('b1', 4, 2, True, False), ('c0', 2, 1, False, False), ('c1', 2, 1, True, False), ('c2', 2, 2, False, True), ('c3', 2, 2, True, True))
B_READY = (5.0, 14.0)
TICK = {1: 3.5, 2: 4.1, 4: 5.5, 8: 9.0}


def coded(x):
    largest = jnp.max(jnp.max(jnp.abs(x), axis=0), axis=0, keepdims=True)
    power = jnp.floor(jnp.log2(jnp.maximum(largest, 1e-30)) * STEP) + 1.0
    codes = jnp.round(x * (jnp.exp2(power * (-1.0 / STEP)) * FULL)[None])
    return codes.astype(jnp.int32).astype(jnp.int16), power


def kernel(nz, plan, values, cols, count, weight, out, *scratch):
    (held, in_copy, own_v, own_wt, got_z, got_sib, got_r, in_send, in_recv) = scratch[:9]
    (b_out, b_in, b_send, b_recv) = scratch[-4:]
    stages = []
    for i, (name, items, stride, mirror, near_first) in enumerate(plan):
        stages.append(Stage(items, nz, stride, mirror, near_first, scratch[9 + 8 * i : 17 + 8 * i]))

    fetch = pltpu.make_async_copy(values, held, in_copy)
    fetch.start()
    p = lax.axis_index("cell")
    ray = lax.axis_index("ray")
    n_cell = lax.axis_size("cell")
    z, yl = ray // 2, ray % 2
    odd = p % 2
    chunk = CT * TILE // nz
    half = chunk // 2
    far = 1 - yl

    def at_cell(shift):
        return {"ray": ray, "cell": lax.rem(p + shift + n_cell, n_cell)}

    def at_z(shift):
        return {"ray": lax.rem(z + shift + nz, nz) * 2 + yl, "cell": p}

    sibling = {"ray": ray, "cell": p + 1 - 2 * odd}
    across = {"ray": ray + 1 - 2 * yl, "cell": p}
    r_target = at_cell(2 * odd - 3)
    r_source = at_cell(2 * odd + 1)
    third = at_cell(6 * odd - 3)

    shifts = set()
    for stage in stages:
        for hop in stage.hops:
            shifts.update((hop, -hop))
    peers = [sibling, at_cell(2), at_cell(-2), third, across] + [at_z(d) for d in sorted(shifts)]
    barrier = pltpu.get_barrier_semaphore()
    for peer in peers:
        pl.semaphore_signal(barrier, inc=1, device_id=peer, device_id_type=MESH)

    row_tiles = values.shape[0]
    started = {}
    guard = [None]

    def send(ends, to):
        src, dst, ssem, rsem = ends()
        copy = pltpu.make_async_remote_copy(
            src_ref=src, dst_ref=dst, send_sem=ssem, recv_sem=rsem, device_id=to, device_id_type=MESH
        )
        copy.start()
        started.setdefault(guard[0], []).append(ends)

    def await_recv(dst, ssem, rsem):
        pltpu.make_async_remote_copy(
            src_ref=dst, dst_ref=dst, send_sem=ssem, recv_sem=rsem, device_id=sibling, device_id_type=MESH
        ).wait_recv()

    def placed(t, i):
        slot, live = jnp.int32(0), jnp.int32(0)
        for k in range(K):
            here = jnp.where((cols[k, t] == i) & (k < count[t]), 1, 0)
            slot += k * here
            live += here
        return held[t, slot].astype(jnp.float32) * live.astype(jnp.float32)

    def place(t, carry):
        for i in range(CT):
            own_v[i, pl.ds(pl.multiple_of(t * TILE, TILE), TILE), :] = placed(t, i).astype(jnp.bfloat16)
        return carry

    fetch.wait()
    lax.fori_loop(0, row_tiles, place, 0)
    pl.semaphore_wait(barrier, len(peers))

    for j in range(CT):
        send(lambda j=j: (own_v.at[j], got_z.at[j], in_send.at[j], in_recv.at[j]), at_cell(2))

    def weigh(t, carry):
        spot = pl.ds(pl.multiple_of(t * TILE, TILE), TILE)
        row = weight[pl.ds(t, 1), :]
        for i in range(CT):
            turned = own_v[i, spot, :].astype(jnp.float32).T
            own_wt[i * TILE : (i + 1) * TILE, spot] = (turned * row).astype(jnp.bfloat16)
        return carry

    lax.fori_loop(0, row_tiles, weigh, 0)
    send(lambda: (own_wt, got_r, in_send.at[8], in_recv.at[8]), r_target)

    def multiply(stage, left, pieces):
        part = stage.refs[0]

        def rows(m, carry):
            spot = pl.ds(pl.multiple_of(m * TILE, TILE), TILE)
            lhs = left[spot, :]
            for i in range(0, len(pieces), 2):
                rhs = jnp.concatenate([pieces[i][...], pieces[i + 1][...]], axis=1)
                got = jnp.dot(lhs, rhs, preferred_element_type=jnp.float32)
                for e in (0, 1):
                    tile = got[:, e * TILE : (e + 1) * TILE]
                    if not stage.near_first:
                        part[0, i + e, spot, :] = tile
                        continue
                    for q in range(TILE // half):
                        to = pl.ds(pl.multiple_of(m * (TILE // 2) + q // 2 * half, half), half)
                        part[q % 2, i + e, to, :] = tile[q * half : (q + 1) * half]
            return carry

        lax.fori_loop(0, CT, rows, 0)

    def decoded(buf, m, slot, width, rows):
        first = 16 + slot * rows
        codes = buf[m, first : first + rows, :].astype(jnp.int32).astype(jnp.float32)
        power = buf[m, 0:16, :].astype(jnp.int32).astype(jnp.float32)
        at = slot * (16 // width)
        return codes * (jnp.exp2(power[at : at + 1] * (1.0 / STEP)) * (1.0 / FULL))

    def encode(buf, m, pieces):
        lines = lax.broadcasted_iota(jnp.int32, (16, TILE), 0)
        for slot, x in enumerate(pieces):
            codes, power = coded(x)
            rows = x.shape[0] * x.shape[1]
            buf[m, 16 + slot * rows : 16 + (slot + 1) * rows, :] = codes.reshape(rows, TILE)
            power = jnp.broadcast_to(power, (16, TILE))
            powers = power if slot == 0 else jnp.where(lines >= slot * (16 // len(pieces)), power, powers)
        buf[m, 0:16, :] = powers.astype(jnp.int32).astype(jnp.int16)

    def own_part(stage, dest):
        part = stage.refs[0]
        if stage.near_first:
            return part[yl, :, pl.ds(pl.multiple_of(dest * half, half), half), :]
        return part[0, :, pl.ds(pl.multiple_of(dest * chunk, chunk), chunk), :]

    def arrived(stage, k, s):
        part, sbuf, rbuf, ssem, rsem = stage.refs[:5]
        m, slot, width = stage.place[k, s]
        tall = half if stage.near_first else chunk
        rows = stage.items * tall
        if m not in stage.seen:
            stage.seen.add(m)
            spot = rbuf.at[m, pl.ds(0, 16 + width * rows)]
            await_recv(spot, ssem.at[m], rsem.at[m])
        return decoded(rbuf, m, slot, width, rows).reshape(stage.items, tall, TILE)

    def step(stage, s):
        part, sbuf, rbuf, ssem, rsem = stage.refs[:5]
        for m, hop, members in stage.steps[s]:
            pieces = []
            for k in members:
                x = own_part(stage, lax.rem(z - stage.paths[k][s] + nz, nz))
                pieces.append(x if s == 0 else x + arrived(stage, k, s - 1))
            encode(sbuf, m, pieces)
            size = 16 + len(members) * pieces[0].shape[0] * pieces[0].shape[1]

            def ends(m=m, size=size):
                spot = pl.ds(0, size)
                return sbuf.at[m, spot], rbuf.at[m, spot], ssem.at[m], rsem.at[m]

            send(ends, at_z(hop))

    def summed(stage):
        x = own_part(stage, z)
        for k, path in enumerate(stage.paths):
            x = x + arrived(stage, k, len(path) - 1)
        return x

    def cross(stage):
        part, near_out, near_in, swap = stage.refs[0], stage.refs[5], stage.refs[6], stage.refs[7]
        encode(near_out, 0, [part[far]])
        send(lambda: (near_out, near_in, swap.at[0], swap.at[1]), across)

    def merge(stage):
        part, near_in, swap = stage.refs[0], stage.refs[6], stage.refs[7]
        await_recv(near_in, swap.at[0], swap.at[1])
        rows = stage.items * half * nz
        part[yl] = part[yl] + decoded(near_in, 0, 0, 1, rows).reshape(stage.items, half * nz, TILE)

    def gather(stage):
        total, other, swap = stage.refs[5:]
        x = summed(stage)
        total[0] = x[:, :half]
        total[1] = x[:, half:]
        send(lambda: (total.at[far], other, swap.at[0], swap.at[1]), across)

    def finish(stage):
        if stage.near_first:
            return summed(stage)
        total, other, swap = stage.refs[5:]
        await_recv(other, swap.at[0], swap.at[1])
        return total[yl] + other[...]

    a, b0, b1 = stages[:3]
    visits = stages[3:]
    sib_s = 1 + 2 * odd
    b_s = 3 - 2 * odd

    def start_a():
        multiply(a, own_wt, [own_v.at[j] for j in range(CT)])

    def only(parity, do):
        def guarded():
            guard[0] = parity
            pl.when(odd == parity)(do)
            guard[0] = None

        return guarded

    def start_b(b):
        await_recv(got_r, in_send.at[8], in_recv.at[8])
        multiply(b, got_r, [own_v.at[j] for j in range(CT)])

    def pass_on(j):
        await_recv(got_z.at[j], in_send.at[j], in_recv.at[j])
        send(lambda: (got_z.at[j], got_sib.at[j], in_send.at[4 + j], in_recv.at[4 + j]), sibling)

    def start_c(j):
        await_recv(got_sib.at[j], in_send.at[4 + j], in_recv.at[4 + j])
        multiply(visits[j], own_wt, [got_z.at[j], got_sib.at[j]])

    def finish_a():
        x = finish(a)
        for i in range(CT):
            out[0, 0, :, i * TILE : (i + 1) * TILE] = x[i]

    def finish_b(b):
        b_out[...] = finish(b)
        send(lambda: (b_out, b_in, b_send, b_recv), r_source)

    def take_b():
        await_recv(b_in, b_send, b_recv)
        for i in range(CT):
            out[b_s, 0, :, i * TILE : (i + 1) * TILE] = b_in[i]

    def finish_c(j):
        x = finish(visits[j])
        out[2, 0, :, j * TILE : (j + 1) * TILE] = x[0]
        out[sib_s, 0, :, j * TILE : (j + 1) * TILE] = x[1]

    events = []

    def run(stage, stride, ready, begin, end, parity=None):
        def add(time, event):
            events.append((time, event if parity is None else only(parity, event)))

        add(ready, begin)
        tick = TICK[stride]
        if stage.near_first:
            add(ready + 0.01, functools.partial(cross, stage))
            add(ready + 4.5, functools.partial(merge, stage))
            ready += 4.5
        for s in range(len(stage.steps)):
            add(ready + 0.1 + tick * s, functools.partial(step, stage, s))
        ready += 0.1 + tick * len(stage.steps)
        if not stage.near_first:
            add(ready, functools.partial(gather, stage))
            ready += 3.4
        add(ready, end)
        return ready

    run(a, plan[0][2], 0.0, start_a, finish_a)
    run(b0, plan[1][2], B_READY[0], functools.partial(start_b, b0), functools.partial(finish_b, b0), 0)
    done = run(b1, plan[2][2], B_READY[1], functools.partial(start_b, b1), functools.partial(finish_b, b1), 1)
    events.append((done + 3.4, take_b))
    for j in range(CT):
        ready = 3.0 + 5.1 * (j + 1)
        events.append((ready, functools.partial(pass_on, j)))
        run(visits[j], plan[3 + j][2], ready + 1.7, functools.partial(start_c, j), functools.partial(finish_c, j))
    for _, event in sorted(events, key=lambda e: e[0]):
        event()
    def drain(copies):
        for ends in copies:
            src, dst, ssem, rsem = ends()
            pltpu.make_async_remote_copy(
                src_ref=src, dst_ref=dst, send_sem=ssem, recv_sem=rsem, device_id=sibling, device_id_type=MESH
            ).wait_send()

    for parity, copies in started.items():
        if parity is None:
            drain(copies)
        else:
            pl.when(odd == parity)(functools.partial(drain, copies))


def body(nz, plan, tile_values, tile_cols, tile_count, ray_weight):
    row_tiles = tile_values.shape[0]
    rays = row_tiles * TILE
    chunk = CT * TILE // nz
    bf16, f32 = jnp.bfloat16, jnp.float32
    dma = pltpu.SemaphoreType.DMA
    scratch = [
        pltpu.VMEM((row_tiles, K, TILE, TILE), bf16),
        dma,
        pltpu.VMEM((CT, rays, TILE), bf16),
        pltpu.VMEM((CT * TILE, rays), bf16),
        pltpu.VMEM((CT, rays, TILE), bf16),
        pltpu.VMEM((CT, rays, TILE), bf16),
        pltpu.VMEM((CT * TILE, rays), bf16),
        dma((9,)),
        dma((9,)),
    ]
    half = chunk // 2
    for name, items, stride, mirror, near_first in plan:
        stage = Stage(items, nz, stride, mirror, near_first, None)
        rows = 16 + stage.widest * items * (half if near_first else chunk)
        near = (1, 16 + items * half * nz, TILE)
        scratch += [
            pltpu.VMEM((2, items, half * nz, TILE) if near_first else (1, items, chunk * nz, TILE), f32),
            pltpu.VMEM((stage.count, rows, TILE), jnp.int16),
            pltpu.VMEM((stage.count, rows, TILE), jnp.int16),
            dma((stage.count,)),
            dma((stage.count,)),
            pltpu.VMEM(near, jnp.int16) if near_first else pltpu.VMEM((2, items, half, TILE), f32),
            pltpu.VMEM(near, jnp.int16) if near_first else pltpu.VMEM((items, half, TILE), f32),
            dma((2,)),
        ]
    scratch += [
        pltpu.VMEM((CT, chunk // 2, TILE), f32),
        pltpu.VMEM((CT, chunk // 2, TILE), f32),
        dma,
        dma,
    ]
    vmem, smem = pl.BlockSpec(memory_space=pltpu.VMEM), pl.BlockSpec(memory_space=pltpu.SMEM)
    return pl.pallas_call(
        functools.partial(kernel, nz, plan),
        out_shape=jax.ShapeDtypeStruct((4, 1, chunk // 2, CT * TILE), f32),
        in_specs=[pl.BlockSpec(memory_space=pltpu.HBM), smem, smem, vmem],
        out_specs=vmem,
        scratch_shapes=scratch,
        compiler_params=pltpu.CompilerParams(
            collective_id=0, has_side_effects=True, vmem_limit_bytes=62 << 20
        ),
    )(
        tile_values.reshape(row_tiles, K, TILE, TILE),
        tile_cols.reshape(row_tiles, K).T,
        tile_count.reshape(row_tiles),
        ray_weight.reshape(row_tiles, TILE),
    )


def solution(mesh):
    return jax.shard_map(
        functools.partial(body, mesh.shape["ray"] // 2, PLAN),
        mesh=mesh,
        in_specs=(P("ray", "cell", None, None, None), P("ray", "cell", None), P("ray", "cell"), P("ray")),
        out_specs=P(None, "cell", "ray", None),
        check_vma=False,
    )
```

```python
import functools

import jax
import jax.numpy as jnp
from jax import lax
from jax.experimental import pallas as pl
from jax.experimental.pallas import tpu as pltpu
from jax.sharding import PartitionSpec as P

MESH = pl.DeviceIdType.MESH
TILE = 128
K = 4
CT = 4
FULL = 32700.0
STEP = 64.0


def streams_of(size, stride, mirror):
    found = []
    half = size // 2
    for sign, reach in ((1, half), (-1, size - 1 - half)):
        for rest in range(stride):
            path = [o for o in range(reach, 0, -1) if o % stride == rest % stride]
            if path:
                found.append([o * sign * (-1 if mirror else 1) for o in path])
    return found


class Stage:
    def __init__(self, items, size, stride, mirror, near_first, refs):
        self.items, self.near_first, self.refs = items, near_first, refs
        self.paths = streams_of(size, stride, mirror)
        self.steps = []
        self.place = {}
        self.count = 0
        self.widest = 1
        for s in range(max(len(path) for path in self.paths)):
            groups = {}
            for k, path in enumerate(self.paths):
                if s < len(path):
                    ahead = path[s + 1] if s + 1 < len(path) else 0
                    groups.setdefault(ahead - path[s], []).append(k)
            found = []
            for hop, members in groups.items():
                for slot, k in enumerate(members):
                    self.place[k, s] = (self.count, slot, len(members))
                self.widest = max(self.widest, len(members))
                found.append((self.count, hop, members))
                self.count += 1
            self.steps.append(found)
        self.hops = {hop for found in self.steps for _, hop, _ in found}
        self.seen = set()


PLAN = (
    ('a', 4, 1, False, False),
    ('b0', 4, 1, True, False),
    ('b1', 4, 2, True, False),
    ('c0', 2, 1, False, False),
    ('c1', 2, 2, True, False),
    ('c2', 2, 2, False, True),
    ('c3', 2, 2, True, True),
)
ORDER = (
    "a.begin", "a.s0", "b0.begin", "b0.s0", "pass0", "a.s1", "b0.s1", "c0.begin", "c0.s0", "a.s2", "pass1",
    "c0.s1", "b0.s2", "c1.begin", "c1.s0", "b1.begin", "c0.s2", "a.s3", "b0.s3", "pass2", "b1.s0", "c1.s1",
    "c2.begin", "c2.cross", "a.s4", "c0.s3", "b0.s4", "pass3", "b1.s1", "c1.s2", "c3.begin", "c3.cross",
    "b0.s5", "c2.merge", "c0.s4", "c2.s0", "b1.s2", "b0.s6", "c3.merge", "c3.s0", "c0.s5", "a.s5", "c2.s1",
    "b1.s3", "c0.s6", "c3.s1", "b0.s7", "a.s6", "c2.s2", "b1.gather", "c1.s3", "c0.s7", "a.s7", "b0.gather",
    "c3.s2", "b1.end", "c2.s3", "a.gather", "b0.end", "c0.gather", "c1.gather", "c3.s3", "a.end", "takeb",
    "c2.end", "c1.end", "c0.end", "c3.end",
)


def coded(x):
    largest = jnp.max(jnp.max(jnp.abs(x), axis=0), axis=0, keepdims=True)
    power = jnp.floor(jnp.log2(jnp.maximum(largest, 1e-30)) * STEP) + 1.0
    codes = jnp.round(x * (jnp.exp2(power * (-1.0 / STEP)) * FULL)[None])
    return codes.astype(jnp.int32).astype(jnp.int16), power


def kernel(nz, plan, values, cols, count, weight, out, *scratch):
    (held, in_copy, own_v, own_wt, got_z, got_sib, got_r, in_send, in_recv) = scratch[:9]
    (b_out, b_in, b_send, b_recv) = scratch[-4:]
    stages = []
    for i, (name, items, stride, mirror, near_first) in enumerate(plan):
        stages.append(Stage(items, nz, stride, mirror, near_first, scratch[9 + 8 * i : 17 + 8 * i]))

    fetch = pltpu.make_async_copy(values, held, in_copy)
    fetch.start()
    p = lax.axis_index("cell")
    ray = lax.axis_index("ray")
    n_cell = lax.axis_size("cell")
    z, yl = ray // 2, ray % 2
    odd = p % 2
    chunk = CT * TILE // nz
    half = chunk // 2
    far = 1 - yl

    def at_cell(shift):
        return {"ray": ray, "cell": lax.rem(p + shift + n_cell, n_cell)}

    def at_z(shift):
        return {"ray": lax.rem(z + shift + nz, nz) * 2 + yl, "cell": p}

    sibling = {"ray": ray, "cell": p + 1 - 2 * odd}
    across = {"ray": ray + 1 - 2 * yl, "cell": p}
    r_target = at_cell(2 * odd - 3)
    r_source = at_cell(2 * odd + 1)
    third = at_cell(6 * odd - 3)

    shifts = set()
    for stage in stages:
        for hop in stage.hops:
            shifts.update((hop, -hop))
    peers = [sibling, at_cell(2), at_cell(-2), third, across] + [at_z(d) for d in sorted(shifts)]
    barrier = pltpu.get_barrier_semaphore()
    for peer in peers:
        pl.semaphore_signal(barrier, inc=1, device_id=peer, device_id_type=MESH)

    row_tiles = values.shape[0]
    started = {}
    guard = [None]

    def send(ends, to):
        src, dst, ssem, rsem = ends()
        copy = pltpu.make_async_remote_copy(
            src_ref=src, dst_ref=dst, send_sem=ssem, recv_sem=rsem, device_id=to, device_id_type=MESH
        )
        copy.start()
        started.setdefault(guard[0], []).append(ends)

    def await_recv(dst, ssem, rsem):
        pltpu.make_async_remote_copy(
            src_ref=dst, dst_ref=dst, send_sem=ssem, recv_sem=rsem, device_id=sibling, device_id_type=MESH
        ).wait_recv()

    def placed(t, i):
        slot, live = jnp.int32(0), jnp.int32(0)
        for k in range(K):
            here = jnp.where((cols[k, t] == i) & (k < count[t]), 1, 0)
            slot += k * here
            live += here
        return held[t, slot].astype(jnp.float32) * live.astype(jnp.float32)

    def place(t, carry):
        for i in range(CT):
            own_v[i, pl.ds(pl.multiple_of(t * TILE, TILE), TILE), :] = placed(t, i).astype(jnp.bfloat16)
        return carry

    fetch.wait()
    lax.fori_loop(0, row_tiles, place, 0)
    pl.semaphore_wait(barrier, len(peers))

    for j in range(CT):
        send(lambda j=j: (own_v.at[j], got_z.at[j], in_send.at[j], in_recv.at[j]), at_cell(2))

    def weigh(t, carry):
        spot = pl.ds(pl.multiple_of(t * TILE, TILE), TILE)
        row = weight[pl.ds(t, 1), :]
        for i in range(CT):
            turned = own_v[i, spot, :].astype(jnp.float32).T
            own_wt[i * TILE : (i + 1) * TILE, spot] = (turned * row).astype(jnp.bfloat16)
        return carry

    lax.fori_loop(0, row_tiles, weigh, 0)
    send(lambda: (own_wt, got_r, in_send.at[8], in_recv.at[8]), r_target)

    def multiply(stage, left, pieces):
        part = stage.refs[0]

        def rows(m, carry):
            spot = pl.ds(pl.multiple_of(m * TILE, TILE), TILE)
            lhs = left[spot, :]
            for i in range(0, len(pieces), 2):
                rhs = jnp.concatenate([pieces[i][...], pieces[i + 1][...]], axis=1)
                got = jnp.dot(lhs, rhs, preferred_element_type=jnp.float32)
                for e in (0, 1):
                    tile = got[:, e * TILE : (e + 1) * TILE]
                    if not stage.near_first:
                        part[0, i + e, spot, :] = tile
                        continue
                    for q in range(TILE // half):
                        to = pl.ds(pl.multiple_of(m * (TILE // 2) + q // 2 * half, half), half)
                        part[q % 2, i + e, to, :] = tile[q * half : (q + 1) * half]
            return carry

        lax.fori_loop(0, CT, rows, 0)

    def decoded(buf, m, slot, width, rows):
        first = 16 + slot * rows
        codes = buf[m, first : first + rows, :].astype(jnp.int32).astype(jnp.float32)
        power = buf[m, 0:16, :].astype(jnp.int32).astype(jnp.float32)
        at = slot * (16 // width)
        return codes * (jnp.exp2(power[at : at + 1] * (1.0 / STEP)) * (1.0 / FULL))

    def encode(buf, m, pieces):
        lines = lax.broadcasted_iota(jnp.int32, (16, TILE), 0)
        for slot, x in enumerate(pieces):
            codes, power = coded(x)
            rows = x.shape[0] * x.shape[1]
            buf[m, 16 + slot * rows : 16 + (slot + 1) * rows, :] = codes.reshape(rows, TILE)
            power = jnp.broadcast_to(power, (16, TILE))
            powers = power if slot == 0 else jnp.where(lines >= slot * (16 // len(pieces)), power, powers)
        buf[m, 0:16, :] = powers.astype(jnp.int32).astype(jnp.int16)

    def own_part(stage, dest):
        part = stage.refs[0]
        if stage.near_first:
            return part[yl, :, pl.ds(pl.multiple_of(dest * half, half), half), :]
        return part[0, :, pl.ds(pl.multiple_of(dest * chunk, chunk), chunk), :]

    def arrived(stage, k, s):
        part, sbuf, rbuf, ssem, rsem = stage.refs[:5]
        m, slot, width = stage.place[k, s]
        tall = half if stage.near_first else chunk
        rows = stage.items * tall
        if m not in stage.seen:
            stage.seen.add(m)
            spot = rbuf.at[m, pl.ds(0, 16 + width * rows)]
            await_recv(spot, ssem.at[m], rsem.at[m])
        return decoded(rbuf, m, slot, width, rows).reshape(stage.items, tall, TILE)

    def step(stage, s):
        part, sbuf, rbuf, ssem, rsem = stage.refs[:5]
        for m, hop, members in stage.steps[s]:
            pieces = []
            for k in members:
                x = own_part(stage, lax.rem(z - stage.paths[k][s] + nz, nz))
                pieces.append(x if s == 0 else x + arrived(stage, k, s - 1))
            encode(sbuf, m, pieces)
            size = 16 + len(members) * pieces[0].shape[0] * pieces[0].shape[1]

            def ends(m=m, size=size):
                spot = pl.ds(0, size)
                return sbuf.at[m, spot], rbuf.at[m, spot], ssem.at[m], rsem.at[m]

            send(ends, at_z(hop))

    def summed(stage):
        x = own_part(stage, z)
        for k, path in enumerate(stage.paths):
            x = x + arrived(stage, k, len(path) - 1)
        return x

    def cross(stage):
        part, near_out, near_in, swap = stage.refs[0], stage.refs[5], stage.refs[6], stage.refs[7]
        encode(near_out, 0, [part[far]])
        send(lambda: (near_out, near_in, swap.at[0], swap.at[1]), across)

    def merge(stage):
        part, near_in, swap = stage.refs[0], stage.refs[6], stage.refs[7]
        await_recv(near_in, swap.at[0], swap.at[1])
        rows = stage.items * half * nz
        part[yl] = part[yl] + decoded(near_in, 0, 0, 1, rows).reshape(stage.items, half * nz, TILE)

    def gather(stage):
        total, other, swap = stage.refs[5:]
        x = summed(stage)
        total[0] = x[:, :half]
        total[1] = x[:, half:]
        send(lambda: (total.at[far], other, swap.at[0], swap.at[1]), across)

    def finish(stage):
        if stage.near_first:
            return summed(stage)
        total, other, swap = stage.refs[5:]
        await_recv(other, swap.at[0], swap.at[1])
        return total[yl] + other[...]

    a, b0, b1 = stages[:3]
    visits = stages[3:]
    sib_s = 1 + 2 * odd
    b_s = 3 - 2 * odd

    def start_a():
        multiply(a, own_wt, [own_v.at[j] for j in range(CT)])

    def only(parity, do):
        def guarded():
            guard[0] = parity
            pl.when(odd == parity)(do)
            guard[0] = None

        return guarded

    def start_b(b):
        await_recv(got_r, in_send.at[8], in_recv.at[8])
        multiply(b, got_r, [own_v.at[j] for j in range(CT)])

    def pass_on(j):
        await_recv(got_z.at[j], in_send.at[j], in_recv.at[j])
        send(lambda: (got_z.at[j], got_sib.at[j], in_send.at[4 + j], in_recv.at[4 + j]), sibling)

    def start_c(j):
        await_recv(got_sib.at[j], in_send.at[4 + j], in_recv.at[4 + j])
        multiply(visits[j], own_wt, [got_z.at[j], got_sib.at[j]])

    def finish_a():
        x = finish(a)
        for i in range(CT):
            out[0, 0, :, i * TILE : (i + 1) * TILE] = x[i]

    def finish_b(b):
        b_out[...] = finish(b)
        send(lambda: (b_out, b_in, b_send, b_recv), r_source)

    def take_b():
        await_recv(b_in, b_send, b_recv)
        for i in range(CT):
            out[b_s, 0, :, i * TILE : (i + 1) * TILE] = b_in[i]

    def finish_c(j):
        x = finish(visits[j])
        out[2, 0, :, j * TILE : (j + 1) * TILE] = x[0]
        out[sib_s, 0, :, j * TILE : (j + 1) * TILE] = x[1]

    events = {}

    def add(name, stage, begin, end, parity=None):
        found = {"begin": begin, "end": end}
        if stage.near_first:
            found["cross"] = functools.partial(cross, stage)
            found["merge"] = functools.partial(merge, stage)
        else:
            found["gather"] = functools.partial(gather, stage)
        for s in range(len(stage.steps)):
            found[f"s{s}"] = functools.partial(step, stage, s)
        for key, event in found.items():
            events[f"{name}.{key}"] = event if parity is None else only(parity, event)

    add("a", a, start_a, finish_a)
    add("b0", b0, functools.partial(start_b, b0), functools.partial(finish_b, b0), 0)
    add("b1", b1, functools.partial(start_b, b1), functools.partial(finish_b, b1), 1)
    events["takeb"] = take_b
    for j in range(CT):
        events[f"pass{j}"] = functools.partial(pass_on, j)
        add(f"c{j}", visits[j], functools.partial(start_c, j), functools.partial(finish_c, j))
    for name in ORDER:
        events.pop(name)()
    assert not events

    def drain(copies):
        for ends in copies:
            src, dst, ssem, rsem = ends()
            pltpu.make_async_remote_copy(
                src_ref=src, dst_ref=dst, send_sem=ssem, recv_sem=rsem, device_id=sibling, device_id_type=MESH
            ).wait_send()

    for parity, copies in started.items():
        if parity is None:
            drain(copies)
        else:
            pl.when(odd == parity)(functools.partial(drain, copies))


def body(nz, plan, tile_values, tile_cols, tile_count, ray_weight):
    row_tiles = tile_values.shape[0]
    rays = row_tiles * TILE
    chunk = CT * TILE // nz
    bf16, f32 = jnp.bfloat16, jnp.float32
    dma = pltpu.SemaphoreType.DMA
    scratch = [
        pltpu.VMEM((row_tiles, K, TILE, TILE), bf16),
        dma,
        pltpu.VMEM((CT, rays, TILE), bf16),
        pltpu.VMEM((CT * TILE, rays), bf16),
        pltpu.VMEM((CT, rays, TILE), bf16),
        pltpu.VMEM((CT, rays, TILE), bf16),
        pltpu.VMEM((CT * TILE, rays), bf16),
        dma((9,)),
        dma((9,)),
    ]
    half = chunk // 2
    for name, items, stride, mirror, near_first in plan:
        stage = Stage(items, nz, stride, mirror, near_first, None)
        rows = 16 + stage.widest * items * (half if near_first else chunk)
        near = (1, 16 + items * half * nz, TILE)
        scratch += [
            pltpu.VMEM((2, items, half * nz, TILE) if near_first else (1, items, chunk * nz, TILE), f32),
            pltpu.VMEM((stage.count, rows, TILE), jnp.int16),
            pltpu.VMEM((stage.count, rows, TILE), jnp.int16),
            dma((stage.count,)),
            dma((stage.count,)),
            pltpu.VMEM(near, jnp.int16) if near_first else pltpu.VMEM((2, items, half, TILE), f32),
            pltpu.VMEM(near, jnp.int16) if near_first else pltpu.VMEM((items, half, TILE), f32),
            dma((2,)),
        ]
    scratch += [
        pltpu.VMEM((CT, chunk // 2, TILE), f32),
        pltpu.VMEM((CT, chunk // 2, TILE), f32),
        dma,
        dma,
    ]
    vmem, smem = pl.BlockSpec(memory_space=pltpu.VMEM), pl.BlockSpec(memory_space=pltpu.SMEM)
    return pl.pallas_call(
        functools.partial(kernel, nz, plan),
        out_shape=jax.ShapeDtypeStruct((4, 1, chunk // 2, CT * TILE), f32),
        in_specs=[pl.BlockSpec(memory_space=pltpu.HBM), smem, smem, vmem],
        out_specs=vmem,
        scratch_shapes=scratch,
        compiler_params=pltpu.CompilerParams(
            collective_id=0, has_side_effects=True, vmem_limit_bytes=54144 << 10
        ),
    )(
        tile_values.reshape(row_tiles, K, TILE, TILE),
        tile_cols.reshape(row_tiles, K).T,
        tile_count.reshape(row_tiles),
        ray_weight.reshape(row_tiles, TILE),
    )


def solution(mesh):
    return jax.shard_map(
        functools.partial(body, mesh.shape["ray"] // 2, PLAN),
        mesh=mesh,
        in_specs=(P("ray", "cell", None, None, None), P("ray", "cell", None), P("ray", "cell"), P("ray")),
        out_specs=P(None, "cell", "ray", None),
        check_vma=False,
    )
```

```python
import functools

import jax
import jax.numpy as jnp
from jax import lax
from jax.experimental import pallas as pl
from jax.experimental.pallas import tpu as pltpu
from jax.sharding import PartitionSpec as P

MESH = pl.DeviceIdType.MESH
TILE = 128
K = 4
CT = 4
FULL = 32700.0
STEP = 64.0


def streams_of(size, stride, mirror):
    found = []
    half = size // 2
    for sign, reach in ((1, half), (-1, size - 1 - half)):
        for rest in range(stride):
            path = [o for o in range(reach, 0, -1) if o % stride == rest % stride]
            if path:
                found.append([o * sign * (-1 if mirror else 1) for o in path])
    return found


class Stage:
    def __init__(self, items, size, stride, mirror, near_first, refs):
        self.items, self.near_first, self.refs = items, near_first, refs
        self.paths = streams_of(size, stride, mirror)
        self.steps = []
        self.place = {}
        self.count = [0, 0]
        self.widest = [1, 1]
        for s in range(max(len(path) for path in self.paths)):
            groups = {}
            for k, path in enumerate(self.paths):
                if s < len(path):
                    last = s + 1 == len(path)
                    ahead = 0 if last else path[s + 1]
                    groups.setdefault((ahead - path[s], last and not near_first), []).append(k)
            found = []
            for (hop, split), members in groups.items():
                kind = int(split)
                for slot, k in enumerate(members):
                    self.place[k, s] = (self.count[kind], slot, len(members))
                self.widest[kind] = max(self.widest[kind], len(members))
                found.append((self.count[kind], hop, members, split))
                self.count[kind] += 1
            self.steps.append(found)
        self.hops = {hop for found in self.steps for _, hop, _, _ in found}
        self.split_hops = {hop for found in self.steps for _, hop, _, split in found if split}
        self.seen = set()


PLAN = (
    (None, 1, False, False),
    (None, 1, True, False),
    (None, 2, True, False),
    ((0,), 1, False, False),
    ((1,), 2, True, False),
    ((2,), 2, False, True),
    ((3,), 2, True, True),
)
ORDER = (
    "a.begin", "a.s0", "b0.begin", "b0.s0", "a.lend", "a.s1", "b0.lend", "pass0", "a.s2", "c0.begin", "c0.s0",
    "c0.lend", "b0.s1", "a.s3", "pass1", "b0.s2", "b1.begin", "b1.s0", "c0.s1", "c1.begin", "c1.s0", "b0.s3",
    "c0.s2", "c1.lend", "b1.lend", "pass2", "b1.s1", "c1.s1", "a.s4", "c2.begin", "c2.cross", "c0.s3",
    "pass3", "b0.s4", "b1.s2", "c3.begin", "c3.cross", "a.s5", "b0.s5", "c2.merge", "c0.s4", "c2.s0", "b1.s3",
    "c3.merge", "c3.s0", "b0.s6", "c0.s5", "c2.s1", "c1.s2", "c3.s1", "c2.s2", "b0.s7", "c0.s6", "b1.end",
    "a.s6", "c3.s2", "c0.s7", "c1.s3", "c2.s3", "a.s7", "b0.end", "c3.s3", "takeb", "c0.end", "c1.end",
    "a.end", "c2.end", "c3.end",
)


def items_of(tiles):
    return CT if tiles is None else 2 * len(tiles)


def coded(x):
    largest = jnp.max(jnp.max(jnp.abs(x), axis=0), axis=0, keepdims=True)
    power = jnp.floor(jnp.log2(jnp.maximum(largest, 1e-30)) * STEP) + 1.0
    codes = jnp.round(x * (jnp.exp2(power * (-1.0 / STEP)) * FULL)[None])
    return codes.astype(jnp.int32).astype(jnp.int16), power


def kernel(nz, plan, values, cols, count, weight, out, *scratch):
    (held, in_copy, own_v, own_wt, got_z, got_sib, got_r, in_send, in_recv) = scratch[:9]
    (b_out, b_in, b_send, b_recv) = scratch[-4:]
    stages = []
    for i, (tiles, stride, mirror, near_first) in enumerate(plan):
        refs = scratch[9 + 12 * i : 21 + 12 * i]
        stages.append(Stage(items_of(tiles), nz, stride, mirror, near_first, refs))

    fetch = pltpu.make_async_copy(values, held, in_copy)
    fetch.start()
    p = lax.axis_index("cell")
    ray = lax.axis_index("ray")
    n_cell = lax.axis_size("cell")
    z, yl = ray // 2, ray % 2
    odd = p % 2
    chunk = CT * TILE // nz
    half = chunk // 2
    far = 1 - yl

    def at_cell(shift):
        return {"ray": ray, "cell": lax.rem(p + shift + n_cell, n_cell)}

    def at_z(shift, h):
        return {"ray": lax.rem(z + shift + nz, nz) * 2 + h, "cell": p}

    sibling = {"ray": ray, "cell": p + 1 - 2 * odd}
    across = {"ray": ray + 1 - 2 * yl, "cell": p}
    r_target = at_cell(2 * odd - 3)
    r_source = at_cell(2 * odd + 1)
    third = at_cell(6 * odd - 3)

    shifts, split_shifts = set(), set()
    for stage in stages:
        for hop in stage.hops:
            shifts.update((hop, -hop))
        for hop in stage.split_hops:
            split_shifts.update((hop, -hop))
    peers = [sibling, at_cell(2), at_cell(-2), third, across] + [at_z(d, yl) for d in sorted(shifts)]
    peers += [at_z(d, far) for d in sorted(split_shifts)]
    barrier = pltpu.get_barrier_semaphore()
    for peer in peers:
        pl.semaphore_signal(barrier, inc=1, device_id=peer, device_id_type=MESH)

    row_tiles = values.shape[0]
    started = {}
    guard = [None]

    def send(ends, to):
        src, dst, ssem, rsem = ends()
        copy = pltpu.make_async_remote_copy(
            src_ref=src, dst_ref=dst, send_sem=ssem, recv_sem=rsem, device_id=to, device_id_type=MESH
        )
        copy.start()
        started.setdefault(guard[0], []).append(ends)

    def await_recv(dst, ssem, rsem):
        pltpu.make_async_remote_copy(
            src_ref=dst, dst_ref=dst, send_sem=ssem, recv_sem=rsem, device_id=sibling, device_id_type=MESH
        ).wait_recv()

    def placed(t, i):
        slot, live = jnp.int32(0), jnp.int32(0)
        for k in range(K):
            here = jnp.where((cols[k, t] == i) & (k < count[t]), 1, 0)
            slot += k * here
            live += here
        return held[t, slot].astype(jnp.float32) * live.astype(jnp.float32)

    def place(t, carry):
        for i in range(CT):
            own_v[i, pl.ds(pl.multiple_of(t * TILE, TILE), TILE), :] = placed(t, i).astype(jnp.bfloat16)
        return carry

    fetch.wait()
    lax.fori_loop(0, row_tiles, place, 0)
    pl.semaphore_wait(barrier, len(peers))

    for j in range(CT):
        send(lambda j=j: (own_v.at[j], got_z.at[j], in_send.at[j], in_recv.at[j]), at_cell(2))

    def weigh(t, carry):
        spot = pl.ds(pl.multiple_of(t * TILE, TILE), TILE)
        row = weight[pl.ds(t, 1), :]
        for i in range(CT):
            turned = own_v[i, spot, :].astype(jnp.float32).T
            own_wt[i * TILE : (i + 1) * TILE, spot] = (turned * row).astype(jnp.bfloat16)
        return carry

    lax.fori_loop(0, row_tiles, weigh, 0)
    send(lambda: (own_wt, got_r, in_send.at[8], in_recv.at[8]), r_target)

    def multiply(stage, left, pieces):
        part = stage.refs[0]

        def rows(m, carry):
            spot = pl.ds(pl.multiple_of(m * TILE, TILE), TILE)
            lhs = left[spot, :]
            for i in range(0, len(pieces), 2):
                rhs = jnp.concatenate([pieces[i][...], pieces[i + 1][...]], axis=1)
                got = jnp.dot(lhs, rhs, preferred_element_type=jnp.float32)
                for e in (0, 1):
                    tile = got[:, e * TILE : (e + 1) * TILE]
                    if not stage.near_first:
                        part[0, i + e, spot, :] = tile
                        continue
                    for q in range(TILE // half):
                        to = pl.ds(pl.multiple_of(m * (TILE // 2) + q // 2 * half, half), half)
                        part[q % 2, i + e, to, :] = tile[q * half : (q + 1) * half]
            return carry

        lax.fori_loop(0, CT, rows, 0)

    def decoded(buf, m, slot, width, rows):
        first = 16 + slot * rows
        codes = buf[m, first : first + rows, :].astype(jnp.int32).astype(jnp.float32)
        power = buf[m, 0:16, :].astype(jnp.int32).astype(jnp.float32)
        at = slot * (16 // width)
        return codes * (jnp.exp2(power[at : at + 1] * (1.0 / STEP)) * (1.0 / FULL))

    def encode(buf, m, pieces):
        lines = lax.broadcasted_iota(jnp.int32, (16, TILE), 0)
        for slot, x in enumerate(pieces):
            codes, power = coded(x)
            rows = x.shape[0] * x.shape[1]
            buf[m, 16 + slot * rows : 16 + (slot + 1) * rows, :] = codes.reshape(rows, TILE)
            power = jnp.broadcast_to(power, (16, TILE))
            powers = power if slot == 0 else jnp.where(lines >= slot * (16 // len(pieces)), power, powers)
        buf[m, 0:16, :] = powers.astype(jnp.int32).astype(jnp.int16)

    def own_part(stage, dest):
        part = stage.refs[0]
        if stage.near_first:
            return part[yl, :, pl.ds(pl.multiple_of(dest * half, half), half), :]
        return part[0, :, pl.ds(pl.multiple_of(dest * chunk, chunk), chunk), :]

    def arrived(stage, k, s):
        rbuf, ssem, rsem = stage.refs[2:5]
        m, slot, width = stage.place[k, s]
        tall = half if stage.near_first else chunk
        rows = stage.items * tall
        if m not in stage.seen:
            stage.seen.add(m)
            spot = rbuf.at[m, pl.ds(0, 16 + width * rows)]
            await_recv(spot, ssem.at[m], rsem.at[m])
        return decoded(rbuf, m, slot, width, rows).reshape(stage.items, tall, TILE)

    def step(stage, s):
        part, sbuf, rbuf, ssem, rsem = stage.refs[:5]
        split_out, split_in, split_send, split_recv = stage.refs[8:]
        for m, hop, members, split in stage.steps[s]:
            pieces = []
            for k in members:
                x = own_part(stage, lax.rem(z - stage.paths[k][s] + nz, nz))
                pieces.append(x if s == 0 else x + arrived(stage, k, s - 1))
            tall = half if split else pieces[0].shape[1]
            size = 16 + len(members) * stage.items * tall
            if not split:
                encode(sbuf, m, pieces)

                def ends(m=m, size=size):
                    spot = pl.ds(0, size)
                    return sbuf.at[m, spot], rbuf.at[m, spot], ssem.at[m], rsem.at[m]

                send(ends, at_z(hop, yl))
                continue
            for h in (0, 1):
                encode(split_out, 2 * m + h, [x[:, h * half : (h + 1) * half] for x in pieces])

                def ends(m=m, size=size, h=h):
                    spot, to = pl.ds(0, size), 2 * m + yl
                    return split_out.at[2 * m + h, spot], split_in.at[to, spot], split_send.at[2 * m + h], split_recv.at[to]

                send(ends, at_z(hop, h))

    def lend(stage):
        part, other, swap = stage.refs[0], stage.refs[5], stage.refs[7]

        def ends():
            rows = pl.ds(pl.multiple_of(z * chunk + far * half, half), half)
            return part.at[0, :, rows, :], other, swap.at[0], swap.at[1]

        send(ends, across)

    def finish(stage):
        part, other, swap = stage.refs[0], stage.refs[5], stage.refs[7]
        if stage.near_first:
            x = own_part(stage, z)
            for k, path in enumerate(stage.paths):
                x = x + arrived(stage, k, len(path) - 1)
            return x
        split_in, split_send, split_recv = stage.refs[9:]
        await_recv(other, swap.at[0], swap.at[1])
        x = part[0, :, pl.ds(pl.multiple_of(z * chunk + yl * half, half), half), :] + other[...]
        rows = stage.items * half
        for k, path in enumerate(stage.paths):
            m, slot, width = stage.place[k, len(path) - 1]
            for side in (0, 1):
                at = 2 * m + side
                if ("split", at) not in stage.seen:
                    stage.seen.add(("split", at))
                    spot = split_in.at[at, pl.ds(0, 16 + width * rows)]
                    await_recv(spot, split_send.at[at], split_recv.at[at])
                x = x + decoded(split_in, at, slot, width, rows).reshape(stage.items, half, TILE)
        return x

    def cross(stage):
        part, near_out, near_in, swap = stage.refs[0], stage.refs[5], stage.refs[6], stage.refs[7]
        encode(near_out, 0, [part[far]])
        send(lambda: (near_out, near_in, swap.at[0], swap.at[1]), across)

    def merge(stage):
        part, near_in, swap = stage.refs[0], stage.refs[6], stage.refs[7]
        await_recv(near_in, swap.at[0], swap.at[1])
        rows = stage.items * half * nz
        part[yl] = part[yl] + decoded(near_in, 0, 0, 1, rows).reshape(stage.items, half * nz, TILE)

    a, b0, b1 = stages[:3]
    visits = stages[3:]
    sib_s = 1 + 2 * odd
    b_s = 3 - 2 * odd

    def start_a():
        multiply(a, own_wt, [own_v.at[j] for j in range(CT)])

    def only(parity, do):
        def guarded():
            guard[0] = parity
            pl.when(odd == parity)(do)
            guard[0] = None

        return guarded

    def start_b(b):
        await_recv(got_r, in_send.at[8], in_recv.at[8])
        multiply(b, got_r, [own_v.at[j] for j in range(CT)])

    def pass_on(j):
        await_recv(got_z.at[j], in_send.at[j], in_recv.at[j])
        send(lambda: (got_z.at[j], got_sib.at[j], in_send.at[4 + j], in_recv.at[4 + j]), sibling)

    def start_c(stage, tiles):
        for j in tiles:
            await_recv(got_sib.at[j], in_send.at[4 + j], in_recv.at[4 + j])
        multiply(stage, own_wt, [got.at[j] for j in tiles for got in (got_z, got_sib)])

    def finish_a():
        x = finish(a)
        for i in range(CT):
            out[0, 0, :, i * TILE : (i + 1) * TILE] = x[i]

    def finish_b(b):
        b_out[...] = finish(b)
        send(lambda: (b_out, b_in, b_send, b_recv), r_source)

    def take_b():
        await_recv(b_in, b_send, b_recv)
        for i in range(CT):
            out[b_s, 0, :, i * TILE : (i + 1) * TILE] = b_in[i]

    def finish_c(stage, tiles):
        x = finish(stage)
        for i, j in enumerate(tiles):
            out[2, 0, :, j * TILE : (j + 1) * TILE] = x[2 * i]
            out[sib_s, 0, :, j * TILE : (j + 1) * TILE] = x[2 * i + 1]

    events = {}

    def add(name, stage, begin, end, parity=None):
        found = {"begin": begin, "end": end}
        if stage.near_first:
            found["cross"] = functools.partial(cross, stage)
            found["merge"] = functools.partial(merge, stage)
        else:
            found["lend"] = functools.partial(lend, stage)
        for s in range(len(stage.steps)):
            found[f"s{s}"] = functools.partial(step, stage, s)
        for key, event in found.items():
            events[f"{name}.{key}"] = event if parity is None else only(parity, event)

    add("a", a, start_a, finish_a)
    add("b0", b0, functools.partial(start_b, b0), functools.partial(finish_b, b0), 0)
    add("b1", b1, functools.partial(start_b, b1), functools.partial(finish_b, b1), 1)
    events["takeb"] = take_b
    for j in range(CT):
        events[f"pass{j}"] = functools.partial(pass_on, j)
    for stage, (tiles, _, _, _) in zip(visits, plan[3:]):
        name = "c" + "".join(map(str, tiles))
        add(name, stage, functools.partial(start_c, stage, tiles), functools.partial(finish_c, stage, tiles))
    for name in ORDER:
        events.pop(name)()
    assert not events

    def drain(copies):
        for ends in copies:
            src, dst, ssem, rsem = ends()
            pltpu.make_async_remote_copy(
                src_ref=src, dst_ref=dst, send_sem=ssem, recv_sem=rsem, device_id=sibling, device_id_type=MESH
            ).wait_send()

    for parity, copies in started.items():
        if parity is None:
            drain(copies)
        else:
            pl.when(odd == parity)(functools.partial(drain, copies))


def body(nz, plan, tile_values, tile_cols, tile_count, ray_weight):
    row_tiles = tile_values.shape[0]
    rays = row_tiles * TILE
    chunk = CT * TILE // nz
    bf16, f32 = jnp.bfloat16, jnp.float32
    dma = pltpu.SemaphoreType.DMA
    scratch = [
        pltpu.VMEM((row_tiles, K, TILE, TILE), bf16),
        dma,
        pltpu.VMEM((CT, rays, TILE), bf16),
        pltpu.VMEM((CT * TILE, rays), bf16),
        pltpu.VMEM((CT, rays, TILE), bf16),
        pltpu.VMEM((CT, rays, TILE), bf16),
        pltpu.VMEM((CT * TILE, rays), bf16),
        dma((9,)),
        dma((9,)),
    ]
    half = chunk // 2
    for tiles, stride, mirror, near_first in plan:
        items = items_of(tiles)
        stage = Stage(items, nz, stride, mirror, near_first, None)
        count, splits = stage.count[0], max(stage.count[1], 1)
        rows = 16 + stage.widest[0] * items * (half if near_first else chunk)
        near = (1, 16 + items * half * nz, TILE)
        split = (2 * splits, 16 + stage.widest[1] * items * half, TILE)
        scratch += [
            pltpu.VMEM((2, items, half * nz, TILE) if near_first else (1, items, chunk * nz, TILE), f32),
            pltpu.VMEM((count, rows, TILE), jnp.int16),
            pltpu.VMEM((count, rows, TILE), jnp.int16),
            dma((count,)),
            dma((count,)),
            pltpu.VMEM(near, jnp.int16) if near_first else pltpu.VMEM((items, half, TILE), f32),
            pltpu.VMEM(near, jnp.int16),
            dma((2,)),
            pltpu.VMEM(split, jnp.int16),
            pltpu.VMEM(split, jnp.int16),
            dma((2 * splits,)),
            dma((2 * splits,)),
        ]
    scratch += [
        pltpu.VMEM((CT, chunk // 2, TILE), f32),
        pltpu.VMEM((CT, chunk // 2, TILE), f32),
        dma,
        dma,
    ]
    vmem, smem = pl.BlockSpec(memory_space=pltpu.VMEM), pl.BlockSpec(memory_space=pltpu.SMEM)
    return pl.pallas_call(
        functools.partial(kernel, nz, plan),
        out_shape=jax.ShapeDtypeStruct((4, 1, chunk // 2, CT * TILE), f32),
        in_specs=[pl.BlockSpec(memory_space=pltpu.HBM), smem, smem, vmem],
        out_specs=vmem,
        scratch_shapes=scratch,
        compiler_params=pltpu.CompilerParams(
            collective_id=0, has_side_effects=True, vmem_limit_bytes=54144 << 10
        ),
    )(
        tile_values.reshape(row_tiles, K, TILE, TILE),
        tile_cols.reshape(row_tiles, K).T,
        tile_count.reshape(row_tiles),
        ray_weight.reshape(row_tiles, TILE),
    )


def solution(mesh):
    return jax.shard_map(
        functools.partial(body, mesh.shape["ray"] // 2, PLAN),
        mesh=mesh,
        in_specs=(P("ray", "cell", None, None, None), P("ray", "cell", None), P("ray", "cell"), P("ray")),
        out_specs=P(None, "cell", "ray", None),
        check_vma=False,
    )
```
